768 devices in a mesh: fsdp: 96 (over z, x, core), tp: 8 (over y).
Axes of the slice: x: 4, y: 8, z: 12, core: 2. Of those that a mesh axis runs over, the one named last changes fastest.
Arguments:
- tokens: bfloat16 [12288, 3584], P('fsdp'), may hold values from -6 to 6
- cotangent: bfloat16 [12288, 14336], P('fsdp', 'tp'), may hold values from -6 to 6
- w_blocks: bfloat16 [96, 8, 3, 128, 128], P('fsdp', 'tp'), may hold values from -0.125 to 0.125
- blk_rows: int32 [96, 8, 3], P('fsdp', 'tp'), may hold values from 0 to 27, as said below
- blk_cols: int32 [96, 8, 3], P('fsdp', 'tp'), may hold values from 0 to 13, as said below
- counts: int32 [96, 8], P('fsdp', 'tp'), may hold values from 1 to 3, as said below
Outputs:
- hidden: bfloat16 [12288, 14336], P('fsdp', 'tp')
- input_grad: bfloat16 [12288, 3584], P('fsdp', 'tp')
The draws below stay inside these ranges and needn't reach their ends.
Inputs may be any that keep to these rules, and one draw needn't show every extreme that they name: `blk_rows`: within one column shard t no two slots, live or not, name the same block. `blk_cols`: block columns within the shard, see blk_rows. `counts`: in every column shard some owner has all 3 slots live.
All inputs are finite; a program needn't handle non-finite values.
Results may differ from the reference program's by a relative error of at most 0.017.
Values may be sent and summed in bfloat16 or wider, within the bound.
No kernel may reach another device: no remote copies, remote signals or barrier semaphores. Data moves between devices by JAX's collectives and lax.ppermute only.
A program may use at most 128 MiB of HBM per device.

```python
import math
import jax
import jax.numpy as jnp
from jax import lax

BLK = 128
D = 3584
FF = 14336
CAP = 3
TOK_DEV = 128
TOKENS = 12288
DB = 28
FBT = 14
N_FSDP = 96
N_TP = 8


def block_positions(key):
    subkeys = jax.random.split(key, N_TP)
    last_position = DB * FBT - 1
    needed = N_FSDP * CAP

    def one_order(subkey):
        first_key, second_key = jax.random.split(subkey)
        ordering = jax.random.permutation(first_key, last_position)
        chosen = jnp.concatenate([jnp.full((1,), last_position, jnp.int32), ordering[:needed - 1].astype(jnp.int32)])
        return jax.random.permutation(second_key, chosen)
    ordering = jax.vmap(one_order)(subkeys)
    taken = ordering.reshape(N_TP, N_FSDP, CAP)
    return jnp.transpose(taken, (1, 0, 2)).astype(jnp.int32)


def draw_blk_rows(key, part):
    positions = block_positions(key)
    return (positions // FBT).astype(jnp.int32)


def draw_blk_cols(key, part):
    positions = block_positions(key)
    return (positions % FBT).astype(jnp.int32)


def draw_counts(key, part):
    key = jax.random.fold_in(key, 11)
    count_key, owner_key = jax.random.split(key)
    initial = jax.random.randint(count_key, (N_FSDP, N_TP), 1, CAP + 1)
    chosen_owner = jax.random.randint(owner_key, (1, N_TP), 0, N_FSDP)
    filled = jnp.arange(N_FSDP)[:, None] == chosen_owner
    return jnp.where(filled, CAP, initial).astype(jnp.int32)


def block_levels(key, shape, shards, least, high):
    gain = 1.0
    for position, parts in shards:
        steps = jax.random.uniform(jax.random.fold_in(jax.random.fold_in(key, 6), position), (parts,), jnp.float32, least / len(shards), high / len(shards))
        gain = gain * jnp.repeat(jnp.exp(steps), shape[position] // parts).reshape((-1,) + (1,) * (len(shape) - 1 - position))
    return gain


def noise(stream_key, shape, spread, bound, cuts=(), kind=jnp.bfloat16):
    values = jax.random.normal(stream_key, shape, jnp.float32) * spread
    if len(cuts) > 0:
        values = block_levels(stream_key, shape, cuts, -0.22, 0.18) * values
    return jnp.clip(values, min=-bound, max=bound).astype(kind)


def setup_inputs(seed: int = 0) -> dict:
    arg_keys = jax.random.split(jax.random.key(seed), 7)
    tokens = noise(arg_keys[0], (TOKENS, D), 1.0, 6.0, ((0, 96),))
    cotangent = noise(arg_keys[1], (TOKENS, FF), 1.0, 6.0, ((0, 96), (1, 8)))
    w_blocks = noise(arg_keys[2], (N_FSDP, N_TP, CAP, BLK, BLK), (2 * N_FSDP * BLK // FBT) ** -0.5, 0.125, ((0, 96), (1, 8)))
    blk_rows = draw_blk_rows(jax.random.fold_in(arg_keys[6], 71), 0)
    blk_cols = draw_blk_cols(jax.random.fold_in(arg_keys[6], 71), 0)
    counts = draw_counts(jax.random.fold_in(arg_keys[6], 71), 0)
    return dict(tokens=tokens, cotangent=cotangent, w_blocks=w_blocks, blk_rows=blk_rows, blk_cols=blk_cols, counts=counts)


gelu_scale = math.sqrt(2.0 / math.pi)

def gelu_parts(preact):
    cube = preact * preact * preact
    tangent = jnp.tanh(gelu_scale * (preact + 0.044715 * cube))
    activated = 0.5 * preact * (1.0 + tangent)
    derivative = 0.5 * (1.0 + tangent) + 0.5 * preact * (1.0 - tangent * tangent) * gelu_scale * (1.0 + 3.0 * 0.044715 * preact * preact)
    return (activated, derivative)

def reference(tokens, cotangent, w_blocks, blk_rows, blk_cols, counts):
    slot_index = jnp.arange(CAP, dtype=jnp.int32)
    live_slot = slot_index[None, None, :] < counts[:, :, None]
    masked = jnp.where(live_slot[:, :, :, None, None], w_blocks, jnp.zeros_like(w_blocks))
    shard_index = jnp.broadcast_to(jnp.arange(N_TP, dtype=jnp.int32)[None, :, None], blk_rows.shape)
    global_col = (shard_index * FBT + blk_cols).astype(jnp.int32)
    dense_weight = jnp.zeros((DB, N_TP * FBT, BLK, BLK), jnp.bfloat16)
    dense_weight = dense_weight.at[blk_rows.reshape(-1), global_col.reshape(-1)].set(masked.reshape(-1, BLK, BLK))
    weight = dense_weight.transpose(0, 2, 1, 3).reshape(D, FF)
    shard_width = FF // N_TP

    def token_block(pair):
        token_rows, cot_rows = pair
        preact = jnp.dot(token_rows, weight, preferred_element_type=jnp.float32)
        activated, derivative = gelu_parts(preact)
        dpre = (cot_rows.astype(jnp.float32) * derivative).astype(jnp.bfloat16)
        summed = jnp.zeros((TOK_DEV, D), jnp.float32)
        for shard in range(N_TP):
            piece = lax.dot_general(dpre[:, shard * shard_width:(shard + 1) * shard_width], weight[:, shard * shard_width:(shard + 1) * shard_width], (((1,), (1,)), ((), ())), preferred_element_type=jnp.float32)
            rounded = lax.optimization_barrier(piece.astype(jnp.bfloat16))
            summed = summed + rounded.astype(jnp.float32)
        return (activated.astype(jnp.bfloat16), summed.astype(jnp.bfloat16))
    hidden, input_grad = lax.map(token_block, (tokens.reshape(N_FSDP, TOK_DEV, D), cotangent.reshape(N_FSDP, TOK_DEV, FF)))
    return (hidden.reshape(TOKENS, FF), input_grad.reshape(TOKENS, D))
```

```python
import math

import jax
import jax.numpy as jnp
from jax import lax
from jax.experimental import pallas as pl
from jax.experimental.pallas import tpu as pltpu
from jax.sharding import PartitionSpec as P

gelu_scale = math.sqrt(2.0 / math.pi)

BLK = 128
CAP = 3
META = 16
UNIT = CAP * BLK + META
NX = 4
NZ = 12
NC = 2
PLACES = [(z, x, c) for z in range(NZ) for x in range(NX) for c in range(NC)]


def place(z, x, c):
    return ((z % NZ) * NX + x % NX) * NC + c % NC


def shift(value, move):
    pairs = [(place(*p), place(*move(*p))) for p in PLACES]
    return lax.ppermute(value, "fsdp", pairs)


def up(value):
    return shift(value, lambda z, x, c: (z + 1, x, c))


def down(value):
    return shift(value, lambda z, x, c: (z - 1, x, c))


def apart(value):
    return shift(value, lambda z, x, c: (z + 1 - 2 * c, x, c))


def sibling(value):
    return shift(value, lambda z, x, c: (z, x, 1 - c))


def gelu_parts(preact):
    cube = preact * preact * preact
    tangent = jnp.tanh(gelu_scale * (preact + 0.044715 * cube))
    activated = 0.5 * preact * (1.0 + tangent)
    derivative = 0.5 * (1.0 + tangent) + 0.5 * preact * (1.0 - tangent * tangent) * gelu_scale * (
        1.0 + 3.0 * 0.044715 * preact * preact
    )
    return (activated, derivative)


def pack(w_blocks, blk_rows, blk_cols, counts):
    live = jnp.arange(CAP, dtype=jnp.int32) < counts.reshape(1)
    blocks = jnp.where(live[:, None, None], w_blocks.reshape(CAP, BLK, BLK), jnp.bfloat16(0))
    places = jnp.concatenate([blk_rows.reshape(CAP), blk_cols.reshape(CAP)]).astype(jnp.bfloat16)
    meta = jnp.pad(places[None, :], ((0, META - 1), (0, BLK - 2 * CAP)))
    return jnp.concatenate([blocks.reshape(CAP * BLK, BLK), meta], axis=0)


def places_of(units):
    n = units.shape[0] // UNIT
    return units.reshape(n, UNIT, BLK)[:, CAP * BLK, : 2 * CAP].astype(jnp.int32)


def scatter_kernel(sizes, *refs):
    n = len(sizes)
    places, sources = refs[0], refs[1 : 1 + n]
    dense, sems = refs[2 + n], refs[3 + n]
    base = 0
    for i, size in enumerate(sizes):
        source = sources[i]

        def one(u, _, source=source, base=base, i=i):
            for s in range(CAP):
                at = (base + u) * (2 * CAP) + s
                row = pl.multiple_of(places[at] * BLK, BLK)
                col = pl.multiple_of(places[at + CAP] * BLK, BLK)
                start = pl.multiple_of(u * UNIT + s * BLK, 16)
                pltpu.make_async_copy(
                    source.at[pl.ds(start, BLK), :],
                    dense.at[pl.ds(row, BLK), pl.ds(col, BLK)],
                    sems.at[i],
                ).start()
            return 0

        lax.fori_loop(0, size, one, 0)
        base += size
    for i, size in enumerate(sizes):
        whole = sources[i].at[pl.ds(0, size * CAP * BLK), :]
        pltpu.make_async_copy(whole, whole, sems.at[i]).wait()


def scatter(dense, stacks):
    sizes = [s.shape[0] // UNIT for s in stacks]
    places = jnp.concatenate([places_of(s) for s in stacks], axis=0).reshape(-1)
    n = len(stacks)
    moved = sum(sizes) * CAP * BLK * BLK * 2
    return pl.pallas_call(
        lambda *refs: scatter_kernel(sizes, *refs),
        out_shape=jax.ShapeDtypeStruct(dense.shape, dense.dtype),
        in_specs=[pl.BlockSpec(memory_space=pltpu.SMEM)]
        + [pl.BlockSpec(memory_space=pl.ANY)] * (n + 1),
        out_specs=pl.BlockSpec(memory_space=pl.ANY),
        scratch_shapes=[pltpu.SemaphoreType.DMA((n,))],
        input_output_aliases={n + 1: 0},
        cost_estimate=pl.CostEstimate(flops=0, bytes_accessed=4 * moved, transcendentals=0),
    )(places, *stacks, dense)


def per_device(tokens, cotangent, w_blocks, blk_rows, blk_cols, counts):
    tokens_here, model_width = tokens.shape
    shard = cotangent.shape[1]
    mine = pack(w_blocks, blk_rows, blk_cols, counts)
    by_x = [[place(z, x, c) for x in range(NX)] for z in range(NZ) for c in range(NC)]
    row = lax.all_gather(mine, "fsdp", axis=0, tiled=True, axis_index_groups=by_x)
    dense = jnp.zeros((model_width, shard), jnp.bfloat16)

    above, below = row, row
    held = [row]
    for step in range(5):
        above, below = up(above), down(below)
        held += [above, below]
    far = apart(lax.select(jnp.full(above.shape, lax.axis_index("fsdp") % NC == 0), above, below))
    first, second = held[:7], held[7:] + [far]
    dense = scatter(dense, first + [sibling(jnp.concatenate(first, axis=0))])
    dense = scatter(dense, second + [sibling(jnp.concatenate(second, axis=0))])

    preact = jnp.dot(tokens, dense, preferred_element_type=jnp.float32)
    activated, derivative = gelu_parts(preact)
    dpre = (cotangent.astype(jnp.float32) * derivative).astype(jnp.bfloat16)
    partial_value = lax.dot_general(
        dpre, dense, (((1,), (1,)), ((), ())), preferred_element_type=jnp.float32
    ).astype(jnp.bfloat16)
    n_tp = lax.axis_size("tp")
    pieces = partial_value.reshape(tokens_here, n_tp, model_width // n_tp).transpose(1, 0, 2)
    terms = lax.all_to_all(pieces, "tp", split_axis=0, concat_axis=0, tiled=True)
    summed = jnp.sum(terms.astype(jnp.float32), axis=0).astype(jnp.bfloat16)
    return (activated.astype(jnp.bfloat16), summed)


def solution(mesh):
    return jax.shard_map(
        per_device,
        mesh=mesh,
        in_specs=(
            P("fsdp", None),
            P("fsdp", "tp"),
            P("fsdp", "tp", None, None, None),
            P("fsdp", "tp", None),
            P("fsdp", "tp", None),
            P("fsdp", "tp"),
        ),
        out_specs=(P("fsdp", "tp"), P("fsdp", "tp")),
        check_vma=False,
    )
```

```python
import math

import jax
import jax.numpy as jnp
from jax import lax
from jax.experimental import pallas as pl
from jax.experimental.pallas import tpu as pltpu
from jax.sharding import PartitionSpec as P

gelu_scale = math.sqrt(2.0 / math.pi)

BLK = 128
CAP = 3
META = 16
UNIT = CAP * BLK + META
NX = 4
NZ = 12
NC = 2
PLACES = [(z, x, c) for z in range(NZ) for x in range(NX) for c in range(NC)]


def place(z, x, c):
    return ((z % NZ) * NX + x % NX) * NC + c % NC


def shift(value, move):
    pairs = [(place(*p), place(*move(*p))) for p in PLACES]
    return lax.ppermute(value, "fsdp", pairs)


def up(value):
    return shift(value, lambda z, x, c: (z + 1, x, c))


def down(value):
    return shift(value, lambda z, x, c: (z - 1, x, c))


def apart(value):
    return shift(value, lambda z, x, c: (z + 1 - 2 * c, x, c))


def sibling(value):
    return shift(value, lambda z, x, c: (z, x, 1 - c))


def gelu_parts(preact):
    cube = preact * preact * preact
    tangent = jnp.tanh(gelu_scale * (preact + 0.044715 * cube))
    activated = 0.5 * preact * (1.0 + tangent)
    derivative = 0.5 * (1.0 + tangent) + 0.5 * preact * (1.0 - tangent * tangent) * gelu_scale * (
        1.0 + 3.0 * 0.044715 * preact * preact
    )
    return (activated, derivative)


def pack(w_blocks, blk_rows, blk_cols, counts):
    live = jnp.arange(CAP, dtype=jnp.int32) < counts.reshape(1)
    blocks = jnp.where(live[:, None, None], w_blocks.reshape(CAP, BLK, BLK), jnp.bfloat16(0))
    places = jnp.concatenate([blk_rows.reshape(CAP), blk_cols.reshape(CAP)]).astype(jnp.bfloat16)
    meta = jnp.pad(places[None, :], ((0, META - 1), (0, BLK - 2 * CAP)))
    return jnp.concatenate([blocks.reshape(CAP * BLK, BLK), meta], axis=0)


def fused_kernel(sizes, *refs):
    n = len(sizes)
    sources = refs[:n]
    tokens, cotangent, hidden, pieces = refs[n : n + 4]
    stage, dense, meta, places, dpre, sems, meta_sem = refs[n + 4 :]
    units = sum(sizes)

    def landing(i):
        first = sum(sizes[:i]) * UNIT
        return pltpu.make_async_copy(
            sources[i], stage.at[pl.ds(first, sizes[i] * UNIT), :], sems.at[i]
        )

    for i in range(n):
        landing(i).start()

    chunks, depth, width = dense.shape

    def clear(i, _):
        at = pl.multiple_of(i * 128, 128)
        for j in range(chunks):
            dense[j, pl.ds(at, 128), :] = jnp.zeros((128, width), jnp.bfloat16)
        return 0

    lax.fori_loop(0, depth // 128, clear, 0)
    for i in range(n):
        landing(i).wait()

    def read(u, _):
        at = pl.multiple_of(u * UNIT + CAP * BLK, META)
        rows = stage[pl.ds(at, META), :].astype(jnp.float32).astype(jnp.int32)
        meta[pl.ds(u, 1), :] = rows[:1]
        return 0

    lax.fori_loop(0, units, read, 0, unroll=8)
    fetch = pltpu.make_async_copy(meta, places, meta_sem)
    fetch.start()
    fetch.wait()

    def put(u, _):
        for s in range(CAP):
            row = pl.multiple_of(places[u, s] * BLK, BLK)
            col = places[u, CAP + s]
            chunk = lax.shift_right_logical(col, 1)
            lane = pl.multiple_of(jnp.bitwise_and(col, 1) * BLK, BLK)
            at = pl.multiple_of(u * UNIT + s * BLK, META)
            dense[chunk, pl.ds(row, BLK), pl.ds(lane, BLK)] = stage[pl.ds(at, BLK), :]
        return 0

    lax.fori_loop(0, units, put, 0, unroll=2)

    for j in range(chunks):
        here = slice(j * width, (j + 1) * width)
        preact = jnp.dot(tokens[...], dense[j], preferred_element_type=jnp.float32)
        activated, derivative = gelu_parts(preact)
        hidden[:, here] = activated.astype(jnp.bfloat16)
        dpre[:, here] = (cotangent[:, here].astype(jnp.float32) * derivative).astype(jnp.bfloat16)
    slab = pieces.shape[2]
    for d in range(pieces.shape[0]):
        total = jnp.zeros(pieces.shape[1:], jnp.float32)
        for j in range(chunks):
            total += lax.dot_general(
                dpre[:, j * width : (j + 1) * width],
                dense[j, d * slab : (d + 1) * slab, :],
                (((1,), (1,)), ((), ())),
                preferred_element_type=jnp.float32,
            )
        pieces[d] = total.astype(jnp.bfloat16)


def fused(stacks, tokens, cotangent, n_tp):
    sizes = [s.shape[0] // UNIT for s in stacks]
    n, units = len(sizes), sum(sizes)
    rows, model_width = tokens.shape
    shard = cotangent.shape[1]
    width = 2 * BLK
    vmem = pl.BlockSpec(memory_space=pltpu.VMEM)
    return pl.pallas_call(
        lambda *refs: fused_kernel(sizes, *refs),
        out_shape=(
            jax.ShapeDtypeStruct((rows, shard), jnp.bfloat16),
            jax.ShapeDtypeStruct((n_tp, rows, model_width // n_tp), jnp.bfloat16),
        ),
        in_specs=[pl.BlockSpec(memory_space=pl.ANY)] * n + [vmem, vmem],
        out_specs=(vmem, vmem),
        scratch_shapes=[
            pltpu.VMEM((units * UNIT, BLK), jnp.bfloat16),
            pltpu.VMEM((shard // width, model_width, width), jnp.bfloat16),
            pltpu.VMEM((units, BLK), jnp.int32),
            pltpu.SMEM((units, BLK), jnp.int32),
            pltpu.VMEM((rows, shard), jnp.bfloat16),
            pltpu.SemaphoreType.DMA((n,)),
            pltpu.SemaphoreType.DMA,
        ],
        compiler_params=pltpu.CompilerParams(vmem_limit_bytes=40 * 1024 * 1024),
        cost_estimate=pl.CostEstimate(
            flops=4 * rows * model_width * shard,
            bytes_accessed=2 * units * UNIT * BLK,
            transcendentals=rows * shard,
        ),
    )(*stacks, tokens, cotangent)


def per_device(tokens, cotangent, w_blocks, blk_rows, blk_cols, counts):
    mine = pack(w_blocks, blk_rows, blk_cols, counts)
    by_x = [[place(z, x, c) for x in range(NX)] for z in range(NZ) for c in range(NC)]
    row = lax.all_gather(mine, "fsdp", axis=0, tiled=True, axis_index_groups=by_x)

    above, below = row, row
    held = [row]
    for step in range(5):
        above, below = up(above), down(below)
        held += [above, below]
    far = apart(lax.select(jnp.full(above.shape, lax.axis_index("fsdp") % NC == 0), above, below))
    batches = [held[:5], held[5:9], held[9:]]
    others = [sibling(jnp.concatenate(b, axis=0)) for b in batches] + [sibling(far)]
    hidden, pieces = fused(held + [far] + others, tokens, cotangent, lax.axis_size("tp"))
    terms = lax.all_to_all(pieces, "tp", split_axis=0, concat_axis=0, tiled=True)
    summed = jnp.sum(terms.astype(jnp.float32), axis=0).astype(jnp.bfloat16)
    return (hidden, summed)


def solution(mesh):
    return jax.shard_map(
        per_device,
        mesh=mesh,
        in_specs=(
            P("fsdp", None),
            P("fsdp", "tp"),
            P("fsdp", "tp", None, None, None),
            P("fsdp", "tp", None),
            P("fsdp", "tp", None),
            P("fsdp", "tp"),
        ),
        out_specs=(P("fsdp", "tp"), P("fsdp", "tp")),
        check_vma=False,
    )
```

```python
import math

import jax
import jax.numpy as jnp
from jax import lax
from jax.experimental import pallas as pl
from jax.experimental.pallas import tpu as pltpu
from jax.sharding import PartitionSpec as P

gelu_scale = math.sqrt(2.0 / math.pi)

BLK = 128
CAP = 3
META = 16
UNIT = CAP * BLK + META
SPOT = 8
SPOTS = BLK // SPOT
NX = 4
NZ = 12
NC = 2
PLACES = [(z, x, c) for z in range(NZ) for x in range(NX) for c in range(NC)]


def place(z, x, c):
    return ((z % NZ) * NX + x % NX) * NC + c % NC


def shift(value, move):
    pairs = [(place(*p), place(*move(*p))) for p in PLACES]
    return lax.ppermute(value, "fsdp", pairs)


def up(value):
    return shift(value, lambda z, x, c: (z + 1, x, c))


def down(value):
    return shift(value, lambda z, x, c: (z - 1, x, c))


def apart(value):
    return shift(value, lambda z, x, c: (z + 1 - 2 * c, x, c))


def sibling(value):
    return shift(value, lambda z, x, c: (z, x, 1 - c))


def gelu_parts(preact):
    cube = preact * preact * preact
    tangent = jnp.tanh(gelu_scale * (preact + 0.044715 * cube))
    activated = 0.5 * preact * (1.0 + tangent)
    derivative = 0.5 * (1.0 + tangent) + 0.5 * preact * (1.0 - tangent * tangent) * gelu_scale * (
        1.0 + 3.0 * 0.044715 * preact * preact
    )
    return (activated, derivative)


def pack(w_blocks, blk_rows, blk_cols, counts):
    live = jnp.arange(CAP, dtype=jnp.int32) < counts.reshape(1)
    blocks = jnp.where(live[:, None, None], w_blocks.reshape(CAP, BLK, BLK), jnp.bfloat16(0))
    places = jnp.concatenate([blk_rows.reshape(1, CAP), blk_cols.reshape(1, CAP)], axis=1)
    owner = lax.axis_index("fsdp")
    meta = lax.dynamic_update_slice(
        jnp.zeros((META, BLK), jnp.bfloat16),
        places.astype(jnp.bfloat16),
        (owner // SPOTS, owner % SPOTS * SPOT),
    )
    return jnp.concatenate([blocks.reshape(CAP * BLK, BLK), meta], axis=0)


def read_places(sources, table, places, sem):
    total = jnp.zeros((META, BLK), jnp.float32)
    for source in sources:
        for first in range(0, source.shape[0], UNIT):
            total += source[first + CAP * BLK : first + UNIT, :].astype(jnp.float32)
    table[...] = total[:8].astype(jnp.int32)
    fetch = pltpu.make_async_copy(table, places, sem)
    fetch.start()
    return fetch


def place_of(move, x, s, places):
    dz, other = move
    me = lax.axis_index("fsdp")
    z = lax.shift_right_logical(me, 3) + dz
    z = jnp.where(z < 0, z + NZ, jnp.where(z >= NZ, z - NZ, z))
    owner = (z * NX + x) * NC + jnp.bitwise_xor(jnp.bitwise_and(me, 1), other)
    spot = lax.shift_right_logical(owner, 4)
    lane = jnp.bitwise_and(owner, SPOTS - 1) * SPOT + s
    return pl.multiple_of(places[spot, lane] * BLK, BLK), places[spot, lane + CAP]


def pair(dense, j, rows=slice(None)):
    return jnp.concatenate([dense[2 * j, rows, :], dense[2 * j + 1, rows, :]], axis=1)


def near_kernel(moves, *refs):
    n = len(moves)
    sources, tokens = refs[:n], refs[n]
    dense, preact, mark, table, places, sem = refs[1 + n :]
    fetch = read_places(sources, table, places, sem)
    columns, depth, _ = dense.shape

    def clear(i, _):
        at = pl.multiple_of(i * BLK, BLK)
        for j in range(columns):
            dense[j, pl.ds(at, BLK), :] = jnp.zeros((BLK, BLK), jnp.bfloat16)
        return 0

    lax.fori_loop(0, depth // BLK, clear, 0)
    fetch.wait()
    for source, rows in zip(sources, moves):
        for k, move in enumerate(rows):
            for x in range(NX):
                at = (k * NX + x) * UNIT
                spots = [place_of(move, x, s, places) for s in range(CAP)]
                blocks = [source[at + s * BLK : at + (s + 1) * BLK, :] for s in range(CAP)]
                for (row, col), block in zip(spots, blocks):
                    dense[col, pl.ds(row, BLK), :] = block
    for j in range(columns // 2):
        total = jnp.dot(tokens[...], pair(dense, j), preferred_element_type=jnp.float32)
        preact[2 * j], preact[2 * j + 1] = total[:, :BLK], total[:, BLK:]
    mark[...] = preact[0, :8, :]


def far_kernel(moves, *refs):
    n = len(moves)
    sources = refs[:n]
    tokens, cotangent, preact, _, hidden, pieces, dense = refs[n : 7 + n]
    table, places, dpre, extra, terms, sem = refs[7 + n :]
    fetch = read_places(sources, table, places, sem)
    extra[...] = jnp.zeros_like(extra)
    fetch.wait()
    blocks = [
        source[first + s * BLK : first + (s + 1) * BLK, :]
        for source in sources
        for first in range(0, source.shape[0], UNIT)
        for s in range(CAP)
    ]
    spots = [
        place_of(move, x, s, places)
        for rows in moves
        for move in rows
        for x in range(NX)
        for s in range(CAP)
    ]
    for i, (row, _) in enumerate(spots):
        terms[i] = jnp.dot(
            tokens[:, pl.ds(row, BLK)], blocks[i], preferred_element_type=jnp.float32
        )
    for i, (row, col) in enumerate(spots):
        dense[col, pl.ds(row, BLK), :] = blocks[i]
        extra[col] += terms[i]

    columns = dense.shape[0]
    for j in range(columns):
        here = slice(j * BLK, (j + 1) * BLK)
        activated, derivative = gelu_parts(preact[j] + extra[j])
        hidden[:, here] = activated.astype(jnp.bfloat16)
        dpre[:, here] = (cotangent[:, here].astype(jnp.float32) * derivative).astype(jnp.bfloat16)
    slab = pieces.shape[2]
    for d in range(pieces.shape[0]):
        total = jnp.zeros(pieces.shape[1:], jnp.float32)
        for j in range(columns // 2):
            total += lax.dot_general(
                dpre[:, 2 * j * BLK : 2 * (j + 1) * BLK],
                pair(dense, j, slice(d * slab, (d + 1) * slab)),
                (((1,), (1,)), ((), ())),
                preferred_element_type=jnp.float32,
            )
        pieces[d] = total.astype(jnp.bfloat16)


def specs(*spaces):
    return [pl.BlockSpec(memory_space=s) for s in spaces]


def near(moves, stacks, tokens, shard):
    n, units = len(stacks), sum(s.shape[0] for s in stacks) // UNIT
    stacks = [pltpu.with_memory_space_constraint(s, pltpu.VMEM) for s in stacks]
    rows, model_width = tokens.shape
    columns = shard // BLK
    return pl.pallas_call(
        lambda *refs: near_kernel(moves, *refs),
        out_shape=(
            pltpu.VMEM((columns, model_width, BLK), jnp.bfloat16),
            pltpu.VMEM((columns, rows, BLK), jnp.float32),
            jax.ShapeDtypeStruct((8, BLK), jnp.float32),
        ),
        in_specs=specs(*[pltpu.VMEM] * n, pltpu.VMEM),
        out_specs=specs(pltpu.VMEM, pltpu.VMEM, pltpu.VMEM),
        scratch_shapes=[
            pltpu.VMEM((8, BLK), jnp.int32),
            pltpu.SMEM((8, BLK), jnp.int32),
            pltpu.SemaphoreType.DMA,
        ],
        compiler_params=pltpu.CompilerParams(vmem_limit_bytes=8 * 1024 * 1024),
        cost_estimate=pl.CostEstimate(
            flops=2 * rows * model_width * shard,
            bytes_accessed=2 * units * UNIT * BLK + 4 * model_width * shard,
            transcendentals=0,
        ),
    )(*stacks, tokens)


def far(moves, stacks, tokens, cotangent, preact, dense, n_tp):
    n, units = len(stacks), sum(s.shape[0] for s in stacks) // UNIT
    stacks = [pltpu.with_memory_space_constraint(s, pltpu.VMEM) for s in stacks]
    rows, model_width = tokens.shape
    shard = cotangent.shape[1]
    hidden, pieces, _ = pl.pallas_call(
        lambda *refs: far_kernel(moves, *refs),
        out_shape=(
            jax.ShapeDtypeStruct((rows, shard), jnp.bfloat16),
            jax.ShapeDtypeStruct((n_tp, rows, model_width // n_tp), jnp.bfloat16),
            pltpu.VMEM(dense.shape, jnp.bfloat16),
        ),
        in_specs=specs(*[pltpu.VMEM] * n, *[pltpu.VMEM] * 4),
        out_specs=specs(pltpu.VMEM, pltpu.VMEM, pltpu.VMEM),
        input_output_aliases={n + 3: 2},
        scratch_shapes=[
            pltpu.VMEM((8, BLK), jnp.int32),
            pltpu.SMEM((8, BLK), jnp.int32),
            pltpu.VMEM((rows, shard), jnp.bfloat16),
            pltpu.VMEM(preact.shape, jnp.float32),
            pltpu.VMEM((units * CAP, rows, BLK), jnp.float32),
            pltpu.SemaphoreType.DMA,
        ],
        compiler_params=pltpu.CompilerParams(vmem_limit_bytes=8 * 1024 * 1024),
        cost_estimate=pl.CostEstimate(
            flops=2 * rows * model_width * shard,
            bytes_accessed=2 * units * UNIT * BLK + 2 * model_width * shard,
            transcendentals=rows * shard,
        ),
    )(*stacks, tokens, cotangent, preact, dense)
    return hidden, pieces


def after(value, mark):
    return pl.pallas_call(
        lambda *refs: None,
        out_shape=jax.ShapeDtypeStruct(value.shape, value.dtype),
        in_specs=specs(pl.ANY, pl.ANY),
        out_specs=pl.BlockSpec(memory_space=pl.ANY),
        input_output_aliases={0: 0},
        compiler_params=pltpu.CompilerParams(vmem_limit_bytes=1024 * 1024),
    )(value, mark)


def by_core_kernel(first, second, out, sem):
    core = jnp.bitwise_and(lax.axis_index("fsdp"), 1)

    @pl.when(core == 1)
    def _():
        copy = pltpu.make_async_copy(first, out, sem)
        copy.start()
        copy.wait()

    @pl.when(core == 0)
    def _():
        copy = pltpu.make_async_copy(second, out, sem)
        copy.start()
        copy.wait()


def by_core(first, second):
    return pl.pallas_call(
        by_core_kernel,
        out_shape=jax.ShapeDtypeStruct(first.shape, first.dtype),
        in_specs=specs(pl.ANY, pl.ANY),
        out_specs=pl.BlockSpec(memory_space=pl.ANY),
        scratch_shapes=[pltpu.SemaphoreType.DMA],
        compiler_params=pltpu.CompilerParams(vmem_limit_bytes=1024 * 1024),
    )(first, second)


def per_device(tokens, cotangent, w_blocks, blk_rows, blk_cols, counts):
    mine = pack(w_blocks, blk_rows, blk_cols, counts)
    by_x = [[place(z, x, c) for x in range(NX)] for z in range(NZ) for c in range(NC)]
    row = lax.all_gather(mine, "fsdp", axis=0, tiled=True, axis_index_groups=by_x)

    above, below = row, row
    held, moves = [row], [(0, 0)]
    for step in range(1, NZ // 2):
        above, below = up(above), down(below)
        held += [above, below]
        moves += [(-step, 0), (step, 0)]
    last = apart(by_core(below, above))
    stacks, rows = list(held), [[m] for m in moves]
    for part in (slice(0, 5), slice(5, 9), slice(9, 11)):
        stacks.append(sibling(jnp.concatenate(held[part], axis=0)))
        rows.append([(dz, 1) for dz, _ in moves[part]])
    dense, preact, mark = near(rows, stacks, tokens, cotangent.shape[1])
    last = after(last, mark)
    hidden, pieces = far(
        [[(NZ // 2, 0)], [(NZ // 2, 1)]],
        [last, sibling(last)],
        tokens,
        cotangent,
        preact,
        dense,
        lax.axis_size("tp"),
    )
    terms = lax.all_to_all(pieces, "tp", split_axis=0, concat_axis=0, tiled=True)
    summed = jnp.sum(terms.astype(jnp.float32), axis=0).astype(jnp.bfloat16)
    return (hidden, summed)


def solution(mesh):
    return jax.shard_map(
        per_device,
        mesh=mesh,
        in_specs=(
            P("fsdp", None),
            P("fsdp", "tp"),
            P("fsdp", "tp", None, None, None),
            P("fsdp", "tp", None),
            P("fsdp", "tp", None),
            P("fsdp", "tp"),
        ),
        out_specs=(P("fsdp", "tp"), P("fsdp", "tp")),
        check_vma=False,
    )
```

```python
import math

import jax
import jax.numpy as jnp
from jax import lax
from jax.experimental import pallas as pl
from jax.experimental.pallas import tpu as pltpu
from jax.sharding import PartitionSpec as P

gelu_scale = math.sqrt(2.0 / math.pi)

BLK = 128
CAP = 3
META = 16
UNIT = CAP * BLK + META
SPOT = 8
SPOTS = BLK // SPOT
NX = 4
NZ = 12
NC = 2
PLACES = [(z, x, c) for z in range(NZ) for x in range(NX) for c in range(NC)]


def place(z, x, c):
    return ((z % NZ) * NX + x % NX) * NC + c % NC


def shift(value, move):
    pairs = [(place(*p), place(*move(*p))) for p in PLACES]
    return lax.ppermute(value, "fsdp", pairs)


def up(value):
    return shift(value, lambda z, x, c: (z + 1, x, c))


def down(value):
    return shift(value, lambda z, x, c: (z - 1, x, c))


def apart(value):
    return shift(value, lambda z, x, c: (z + 1 - 2 * c, x, c))


def sibling(value):
    return shift(value, lambda z, x, c: (z, x, 1 - c))


def gelu_parts(preact):
    cube = preact * preact * preact
    tangent = jnp.tanh(gelu_scale * (preact + 0.044715 * cube))
    activated = 0.5 * preact * (1.0 + tangent)
    derivative = 0.5 * (1.0 + tangent) + 0.5 * preact * (1.0 - tangent * tangent) * gelu_scale * (
        1.0 + 3.0 * 0.044715 * preact * preact
    )
    return (activated, derivative)


def pack_kernel(blocks, rows, cols, counts, out):
    owner = lax.axis_index("fsdp")
    for s in range(CAP):
        here = slice(s * BLK, (s + 1) * BLK)

        @pl.when(s < counts[0, 0])
        def _(s=s, here=here):
            out[here, :] = blocks[0, 0, s]

        @pl.when(s >= counts[0, 0])
        def _(here=here):
            out[here, :] = jnp.zeros((BLK, BLK), jnp.bfloat16)

    row = lax.broadcasted_iota(jnp.int32, (META, BLK), 0) - lax.shift_right_logical(owner, 4)
    lane = lax.broadcasted_iota(jnp.int32, (META, BLK), 1)
    lane = lane - jnp.bitwise_and(owner, SPOTS - 1) * SPOT
    meta = jnp.zeros((META, BLK), jnp.float32)
    for s in range(CAP):
        for place, at in ((rows[0, 0, s], s), (cols[0, 0, s], s + CAP)):
            meta = jnp.where((row == 0) & (lane == at), place.astype(jnp.float32), meta)
    out[CAP * BLK :, :] = meta.astype(jnp.bfloat16)


def pack(w_blocks, blk_rows, blk_cols, counts):
    return pl.pallas_call(
        pack_kernel,
        out_shape=jax.ShapeDtypeStruct((UNIT, BLK), jnp.bfloat16),
        in_specs=specs(pltpu.VMEM, pltpu.SMEM, pltpu.SMEM, pltpu.SMEM),
        out_specs=pl.BlockSpec(memory_space=pltpu.VMEM),
        compiler_params=pltpu.CompilerParams(vmem_limit_bytes=4 * 1024 * 1024),
    )(w_blocks, blk_rows, blk_cols, counts)


def read_places(sources, table, places, sem):
    total = jnp.zeros((META, BLK), jnp.float32)
    for source in sources:
        for first in range(0, source.shape[0], UNIT):
            total += source[first + CAP * BLK : first + UNIT, :].astype(jnp.float32)
    table[...] = total[:8].astype(jnp.int32)
    fetch = pltpu.make_async_copy(table, places, sem)
    fetch.start()
    return fetch


def place_of(move, x, s, places):
    dz, other = move
    me = lax.axis_index("fsdp")
    z = lax.shift_right_logical(me, 3) + dz
    z = jnp.where(z < 0, z + NZ, jnp.where(z >= NZ, z - NZ, z))
    owner = (z * NX + x) * NC + jnp.bitwise_xor(jnp.bitwise_and(me, 1), other)
    spot = lax.shift_right_logical(owner, 4)
    lane = jnp.bitwise_and(owner, SPOTS - 1) * SPOT + s
    return pl.multiple_of(places[spot, lane] * BLK, BLK), places[spot, lane + CAP]


def pair(dense, j, rows=slice(None)):
    return jnp.concatenate([dense[2 * j, rows, :], dense[2 * j + 1, rows, :]], axis=1)


def near_kernel(moves, *refs):
    n = len(moves)
    sources, tokens = refs[:n], refs[n]
    dense, preact, mark, table, places, sem = refs[1 + n :]
    fetch = read_places(sources, table, places, sem)
    columns, depth, _ = dense.shape

    def clear(i, _):
        at = pl.multiple_of(i * BLK, BLK)
        for j in range(columns):
            dense[j, pl.ds(at, BLK), :] = jnp.zeros((BLK, BLK), jnp.bfloat16)
        return 0

    lax.fori_loop(0, depth // BLK, clear, 0)
    fetch.wait()
    for source, rows in zip(sources, moves):
        for k, move in enumerate(rows):
            for x in range(NX):
                at = (k * NX + x) * UNIT
                spots = [place_of(move, x, s, places) for s in range(CAP)]
                blocks = [source[at + s * BLK : at + (s + 1) * BLK, :] for s in range(CAP)]
                for (row, col), block in zip(spots, blocks):
                    dense[col, pl.ds(row, BLK), :] = block
    for j in range(columns // 2):
        total = jnp.dot(tokens[...], pair(dense, j), preferred_element_type=jnp.float32)
        preact[2 * j], preact[2 * j + 1] = total[:, :BLK], total[:, BLK:]
    mark[...] = preact[0, :8, :]


def far_kernel(moves, *refs):
    n = len(moves)
    sources = refs[:n]
    tokens, cotangent, preact, _, hidden, pieces, dense = refs[n : 7 + n]
    table, places, dpre, extra, terms, sem = refs[7 + n :]
    fetch = read_places(sources, table, places, sem)
    extra[...] = jnp.zeros_like(extra)
    fetch.wait()
    blocks = [
        source[first + s * BLK : first + (s + 1) * BLK, :]
        for source in sources
        for first in range(0, source.shape[0], UNIT)
        for s in range(CAP)
    ]
    spots = [
        place_of(move, x, s, places)
        for rows in moves
        for move in rows
        for x in range(NX)
        for s in range(CAP)
    ]
    for i, (row, _) in enumerate(spots):
        terms[i] = jnp.dot(
            tokens[:, pl.ds(row, BLK)], blocks[i], preferred_element_type=jnp.float32
        )
    for i, (row, col) in enumerate(spots):
        dense[col, pl.ds(row, BLK), :] = blocks[i]
        extra[col] += terms[i]

    columns = dense.shape[0]
    for j in range(columns):
        here = slice(j * BLK, (j + 1) * BLK)
        activated, derivative = gelu_parts(preact[j] + extra[j])
        hidden[:, here] = activated.astype(jnp.bfloat16)
        dpre[:, here] = (cotangent[:, here].astype(jnp.float32) * derivative).astype(jnp.bfloat16)
    slab = pieces.shape[1]
    for d in range(pieces.shape[0]):
        total = jnp.zeros(pieces.shape[1:], jnp.float32)
        for j in range(columns // 2):
            total += lax.dot_general(
                pair(dense, j, slice(d * slab, (d + 1) * slab)),
                dpre[:, 2 * j * BLK : 2 * (j + 1) * BLK],
                (((1,), (1,)), ((), ())),
                preferred_element_type=jnp.float32,
            )
        pieces[d] = total.astype(jnp.bfloat16)


def specs(*spaces):
    return [pl.BlockSpec(memory_space=s) for s in spaces]


def near(moves, stacks, tokens, shard):
    n, units = len(stacks), sum(s.shape[0] for s in stacks) // UNIT
    stacks = [pltpu.with_memory_space_constraint(s, pltpu.VMEM) for s in stacks]
    rows, model_width = tokens.shape
    columns = shard // BLK
    return pl.pallas_call(
        lambda *refs: near_kernel(moves, *refs),
        out_shape=(
            pltpu.VMEM((columns, model_width, BLK), jnp.bfloat16),
            pltpu.VMEM((columns, rows, BLK), jnp.float32),
            jax.ShapeDtypeStruct((8, BLK), jnp.float32),
        ),
        in_specs=specs(*[pltpu.VMEM] * n, pltpu.VMEM),
        out_specs=specs(pltpu.VMEM, pltpu.VMEM, pltpu.VMEM),
        scratch_shapes=[
            pltpu.VMEM((8, BLK), jnp.int32),
            pltpu.SMEM((8, BLK), jnp.int32),
            pltpu.SemaphoreType.DMA,
        ],
        compiler_params=pltpu.CompilerParams(vmem_limit_bytes=8 * 1024 * 1024),
        cost_estimate=pl.CostEstimate(
            flops=2 * rows * model_width * shard,
            bytes_accessed=2 * units * UNIT * BLK + 4 * model_width * shard,
            transcendentals=0,
        ),
    )(*stacks, tokens)


def far(moves, stacks, tokens, cotangent, preact, dense, n_tp):
    n, units = len(stacks), sum(s.shape[0] for s in stacks) // UNIT
    stacks = [pltpu.with_memory_space_constraint(s, pltpu.VMEM) for s in stacks]
    rows, model_width = tokens.shape
    shard = cotangent.shape[1]
    hidden, pieces, _ = pl.pallas_call(
        lambda *refs: far_kernel(moves, *refs),
        out_shape=(
            jax.ShapeDtypeStruct((rows, shard), jnp.bfloat16),
            jax.ShapeDtypeStruct((n_tp, model_width // n_tp, rows), jnp.bfloat16),
            pltpu.VMEM(dense.shape, jnp.bfloat16),
        ),
        in_specs=specs(*[pltpu.VMEM] * n, *[pltpu.VMEM] * 4),
        out_specs=specs(pltpu.VMEM, pltpu.VMEM, pltpu.VMEM),
        input_output_aliases={n + 3: 2},
        scratch_shapes=[
            pltpu.VMEM((8, BLK), jnp.int32),
            pltpu.SMEM((8, BLK), jnp.int32),
            pltpu.VMEM((rows, shard), jnp.bfloat16),
            pltpu.VMEM(preact.shape, jnp.float32),
            pltpu.VMEM((units * CAP, rows, BLK), jnp.float32),
            pltpu.SemaphoreType.DMA,
        ],
        compiler_params=pltpu.CompilerParams(vmem_limit_bytes=8 * 1024 * 1024),
        cost_estimate=pl.CostEstimate(
            flops=2 * rows * model_width * shard,
            bytes_accessed=2 * units * UNIT * BLK + 2 * model_width * shard,
            transcendentals=rows * shard,
        ),
    )(*stacks, tokens, cotangent, preact, dense)
    return hidden, pieces


def after(value, mark):
    return pl.pallas_call(
        lambda *refs: None,
        out_shape=jax.ShapeDtypeStruct(value.shape, value.dtype),
        in_specs=specs(pl.ANY, pl.ANY),
        out_specs=pl.BlockSpec(memory_space=pl.ANY),
        input_output_aliases={0: 0},
        compiler_params=pltpu.CompilerParams(vmem_limit_bytes=1024 * 1024),
    )(value, mark)


def by_core_kernel(first, second, out, _first, _second, sem):
    core = jnp.bitwise_and(lax.axis_index("fsdp"), 1)

    @pl.when(core == 1)
    def _():
        copy = pltpu.make_async_copy(first, out, sem)
        copy.start()
        copy.wait()

    @pl.when(core == 0)
    def _():
        copy = pltpu.make_async_copy(second, out, sem)
        copy.start()
        copy.wait()


def by_core(first, second):
    return pl.pallas_call(
        by_core_kernel,
        out_shape=(jax.ShapeDtypeStruct(first.shape, first.dtype),) * 3,
        in_specs=specs(pl.ANY, pl.ANY),
        out_specs=specs(pl.ANY, pl.ANY, pl.ANY),
        input_output_aliases={0: 1, 1: 2},
        scratch_shapes=[pltpu.SemaphoreType.DMA],
        compiler_params=pltpu.CompilerParams(vmem_limit_bytes=1024 * 1024),
    )(first, second)


def per_device(tokens, cotangent, w_blocks, blk_rows, blk_cols, counts):
    mine = pack(w_blocks, blk_rows, blk_cols, counts)
    by_x = [[place(z, x, c) for x in range(NX)] for z in range(NZ) for c in range(NC)]
    row = lax.all_gather(mine, "fsdp", axis=0, tiled=True, axis_index_groups=by_x)

    above, below = row, row
    held, moves = [row], [(0, 0)]
    for step in range(1, NZ // 2):
        above, below = up(above), down(below)
        held += [above, below]
        moves += [(-step, 0), (step, 0)]
    chosen, below, above = by_core(below, above)
    last = apart(chosen)
    held[-2:] = [above, below]
    stacks, rows = list(held), [[m] for m in moves]
    for part in (slice(0, 5), slice(5, 9), slice(9, 11)):
        stacks.append(sibling(jnp.concatenate(held[part], axis=0)))
        rows.append([(dz, 1) for dz, _ in moves[part]])
    dense, preact, mark = near(rows, stacks, tokens, cotangent.shape[1])
    last = after(last, mark)
    hidden, pieces = far(
        [[(NZ // 2, 0)], [(NZ // 2, 1)]],
        [last, sibling(last)],
        tokens,
        cotangent,
        preact,
        dense,
        lax.axis_size("tp"),
    )
    terms = lax.all_to_all(pieces, "tp", split_axis=0, concat_axis=0, tiled=True)
    summed = jnp.sum(terms.astype(jnp.float32), axis=0).astype(jnp.bfloat16)
    return (hidden, summed.T)


def solution(mesh):
    return jax.shard_map(
        per_device,
        mesh=mesh,
        in_specs=(
            P("fsdp", None),
            P("fsdp", "tp"),
            P("fsdp", "tp", None, None, None),
            P("fsdp", "tp", None),
            P("fsdp", "tp", None),
            P("fsdp", "tp"),
        ),
        out_specs=(P("fsdp", "tp"), P("fsdp", "tp")),
        check_vma=False,
    )
```

```python
import math

import jax
import jax.numpy as jnp
from jax import lax
from jax.experimental import pallas as pl
from jax.experimental.pallas import tpu as pltpu
from jax.sharding import PartitionSpec as P

gelu_scale = math.sqrt(2.0 / math.pi)

BLK = 128
CAP = 3
META = 16
UNIT = CAP * BLK + META
SPOT = 8
SPOTS = BLK // SPOT
NX = 4
NZ = 12
NC = 2
PLACES = [(z, x, c) for z in range(NZ) for x in range(NX) for c in range(NC)]


def place(z, x, c):
    return ((z % NZ) * NX + x % NX) * NC + c % NC


def shift(value, move):
    pairs = [(place(*p), place(*move(*p))) for p in PLACES]
    return lax.ppermute(value, "fsdp", pairs)


def up(value):
    return shift(value, lambda z, x, c: (z + 1, x, c))


def down(value):
    return shift(value, lambda z, x, c: (z - 1, x, c))


def apart(value):
    return shift(value, lambda z, x, c: (z + 1 - 2 * c, x, c))


def sibling(value):
    return shift(value, lambda z, x, c: (z, x, 1 - c))


def gelu_parts(preact):
    cube = preact * preact * preact
    tangent = jnp.tanh(gelu_scale * (preact + 0.044715 * cube))
    activated = 0.5 * preact * (1.0 + tangent)
    derivative = 0.5 * (1.0 + tangent) + 0.5 * preact * (1.0 - tangent * tangent) * gelu_scale * (
        1.0 + 3.0 * 0.044715 * preact * preact
    )
    return (activated, derivative)


def pack_kernel(*refs):
    out, sems = refs[4], refs[9]
    copies = [pltpu.make_async_copy(refs[i], refs[5 + i], sems.at[i]) for i in range(4)]
    for copy in copies:
        copy.start()
    for copy in copies:
        copy.wait()
    blocks, rows, cols, counts = refs[5:9]
    owner = lax.axis_index("fsdp")
    for s in range(CAP):
        here = slice(s * BLK, (s + 1) * BLK)

        @pl.when(s < counts[0, 0])
        def _(s=s, here=here):
            out[here, :] = blocks[0, 0, s]

        @pl.when(s >= counts[0, 0])
        def _(here=here):
            out[here, :] = jnp.zeros((BLK, BLK), jnp.bfloat16)

    row = lax.broadcasted_iota(jnp.int32, (META, BLK), 0) - lax.shift_right_logical(owner, 4)
    lane = lax.broadcasted_iota(jnp.int32, (META, BLK), 1)
    lane = lane - jnp.bitwise_and(owner, SPOTS - 1) * SPOT
    meta = jnp.zeros((META, BLK), jnp.float32)
    for s in range(CAP):
        for place, at in ((rows[0, 0, s], s), (cols[0, 0, s], s + CAP)):
            meta = jnp.where((row == 0) & (lane == at), place.astype(jnp.float32), meta)
    out[CAP * BLK :, :] = meta.astype(jnp.bfloat16)


def pack(w_blocks, blk_rows, blk_cols, counts):
    args = [
        pltpu.with_memory_space_constraint(a, pltpu.HBM)
        for a in (w_blocks, blk_rows, blk_cols)
    ]
    return pl.pallas_call(
        pack_kernel,
        out_shape=jax.ShapeDtypeStruct((UNIT, BLK), jnp.bfloat16),
        in_specs=specs(pltpu.HBM, pltpu.HBM, pltpu.HBM, pl.ANY),
        out_specs=pl.BlockSpec(memory_space=pltpu.VMEM),
        scratch_shapes=[
            pltpu.VMEM(w_blocks.shape, w_blocks.dtype),
            pltpu.SMEM(blk_rows.shape, jnp.int32),
            pltpu.SMEM(blk_cols.shape, jnp.int32),
            pltpu.SMEM(counts.shape, jnp.int32),
            pltpu.SemaphoreType.DMA((4,)),
        ],
        compiler_params=pltpu.CompilerParams(vmem_limit_bytes=8 * 1024 * 1024),
    )(*args, counts)


def read_places(sources, table, places, sem):
    total = jnp.zeros((META, BLK), jnp.float32)
    for source in sources:
        for first in range(0, source.shape[0], UNIT):
            total += source[first + CAP * BLK : first + UNIT, :].astype(jnp.float32)
    table[...] = total[:8].astype(jnp.int32)
    fetch = pltpu.make_async_copy(table, places, sem)
    fetch.start()
    return fetch


def place_of(move, x, s, places):
    dz, other = move
    me = lax.axis_index("fsdp")
    z = lax.shift_right_logical(me, 3) + dz
    z = jnp.where(z < 0, z + NZ, jnp.where(z >= NZ, z - NZ, z))
    owner = (z * NX + x) * NC + jnp.bitwise_xor(jnp.bitwise_and(me, 1), other)
    spot = lax.shift_right_logical(owner, 4)
    lane = jnp.bitwise_and(owner, SPOTS - 1) * SPOT + s
    return pl.multiple_of(places[spot, lane] * BLK, BLK), places[spot, lane + CAP]


def pair(dense, j, rows=slice(None)):
    return jnp.concatenate([dense[2 * j, rows, :], dense[2 * j + 1, rows, :]], axis=1)


def near_kernel(moves, *refs):
    n = len(moves)
    sources, tokens = refs[:n], refs[n]
    dense, preact, mark, table, places, sem = refs[1 + n :]
    fetch = read_places(sources, table, places, sem)
    columns, depth, _ = dense.shape

    def clear(i, _):
        at = pl.multiple_of(i * BLK, BLK)
        for j in range(columns):
            dense[j, pl.ds(at, BLK), :] = jnp.zeros((BLK, BLK), jnp.bfloat16)
        return 0

    lax.fori_loop(0, depth // BLK, clear, 0)
    fetch.wait()
    for source, rows in zip(sources, moves):
        for k, move in enumerate(rows):
            for x in range(NX):
                at = (k * NX + x) * UNIT
                spots = [place_of(move, x, s, places) for s in range(CAP)]
                blocks = [source[at + s * BLK : at + (s + 1) * BLK, :] for s in range(CAP)]
                for (row, col), block in zip(spots, blocks):
                    dense[col, pl.ds(row, BLK), :] = block
    for j in range(columns // 2):
        total = jnp.dot(tokens[...], pair(dense, j), preferred_element_type=jnp.float32)
        preact[2 * j], preact[2 * j + 1] = total[:, :BLK], total[:, BLK:]
    mark[...] = preact[0, :8, :]


def far_kernel(moves, *refs):
    n = len(moves)
    sources = refs[:n]
    tokens, cotangent, preact, _, hidden, pieces, dense = refs[n : 7 + n]
    table, places, dpre, extra, terms, sem = refs[7 + n :]
    fetch = read_places(sources, table, places, sem)
    extra[...] = jnp.zeros_like(extra)
    fetch.wait()
    blocks = [
        source[first + s * BLK : first + (s + 1) * BLK, :]
        for source in sources
        for first in range(0, source.shape[0], UNIT)
        for s in range(CAP)
    ]
    spots = [
        place_of(move, x, s, places)
        for rows in moves
        for move in rows
        for x in range(NX)
        for s in range(CAP)
    ]
    for i, (row, _) in enumerate(spots):
        terms[i] = jnp.dot(
            tokens[:, pl.ds(row, BLK)], blocks[i], preferred_element_type=jnp.float32
        )
    for i, (row, col) in enumerate(spots):
        dense[col, pl.ds(row, BLK), :] = blocks[i]
        extra[col] += terms[i]

    columns = dense.shape[0]
    for j in range(columns):
        here = slice(j * BLK, (j + 1) * BLK)
        activated, derivative = gelu_parts(preact[j] + extra[j])
        hidden[:, here] = activated.astype(jnp.bfloat16)
        dpre[:, here] = (cotangent[:, here].astype(jnp.float32) * derivative).astype(jnp.bfloat16)
    slab = pieces.shape[1]
    for d in range(pieces.shape[0]):
        total = jnp.zeros(pieces.shape[1:], jnp.float32)
        for j in range(columns // 2):
            total += lax.dot_general(
                pair(dense, j, slice(d * slab, (d + 1) * slab)),
                dpre[:, 2 * j * BLK : 2 * (j + 1) * BLK],
                (((1,), (1,)), ((), ())),
                preferred_element_type=jnp.float32,
            )
        pieces[d] = total.astype(jnp.bfloat16)


def specs(*spaces):
    return [pl.BlockSpec(memory_space=s) for s in spaces]


def near(moves, stacks, tokens, shard):
    n, units = len(stacks), sum(s.shape[0] for s in stacks) // UNIT
    stacks = [pltpu.with_memory_space_constraint(s, pltpu.VMEM) for s in stacks]
    rows, model_width = tokens.shape
    columns = shard // BLK
    return pl.pallas_call(
        lambda *refs: near_kernel(moves, *refs),
        out_shape=(
            pltpu.VMEM((columns, model_width, BLK), jnp.bfloat16),
            pltpu.VMEM((columns, rows, BLK), jnp.float32),
            jax.ShapeDtypeStruct((8, BLK), jnp.float32),
        ),
        in_specs=specs(*[pltpu.VMEM] * n, pltpu.VMEM),
        out_specs=specs(pltpu.VMEM, pltpu.VMEM, pltpu.VMEM),
        scratch_shapes=[
            pltpu.VMEM((8, BLK), jnp.int32),
            pltpu.SMEM((8, BLK), jnp.int32),
            pltpu.SemaphoreType.DMA,
        ],
        compiler_params=pltpu.CompilerParams(vmem_limit_bytes=8 * 1024 * 1024),
        cost_estimate=pl.CostEstimate(
            flops=2 * rows * model_width * shard,
            bytes_accessed=2 * units * UNIT * BLK + 4 * model_width * shard,
            transcendentals=0,
        ),
    )(*stacks, tokens)


def far(moves, stacks, tokens, cotangent, preact, dense, n_tp):
    n, units = len(stacks), sum(s.shape[0] for s in stacks) // UNIT
    stacks = [pltpu.with_memory_space_constraint(s, pltpu.VMEM) for s in stacks]
    rows, model_width = tokens.shape
    shard = cotangent.shape[1]
    hidden, pieces, _ = pl.pallas_call(
        lambda *refs: far_kernel(moves, *refs),
        out_shape=(
            jax.ShapeDtypeStruct((rows, shard), jnp.bfloat16),
            jax.ShapeDtypeStruct((n_tp, model_width // n_tp, rows), jnp.bfloat16),
            pltpu.VMEM(dense.shape, jnp.bfloat16),
        ),
        in_specs=specs(*[pltpu.VMEM] * n, *[pltpu.VMEM] * 4),
        out_specs=specs(pltpu.VMEM, pltpu.VMEM, pltpu.VMEM),
        input_output_aliases={n + 3: 2},
        scratch_shapes=[
            pltpu.VMEM((8, BLK), jnp.int32),
            pltpu.SMEM((8, BLK), jnp.int32),
            pltpu.VMEM((rows, shard), jnp.bfloat16),
            pltpu.VMEM(preact.shape, jnp.float32),
            pltpu.VMEM((units * CAP, rows, BLK), jnp.float32),
            pltpu.SemaphoreType.DMA,
        ],
        compiler_params=pltpu.CompilerParams(vmem_limit_bytes=8 * 1024 * 1024),
        cost_estimate=pl.CostEstimate(
            flops=2 * rows * model_width * shard,
            bytes_accessed=2 * units * UNIT * BLK + 2 * model_width * shard,
            transcendentals=rows * shard,
        ),
    )(*stacks, tokens, cotangent, preact, dense)
    return hidden, pieces


def after(value, mark):
    return pl.pallas_call(
        lambda *refs: None,
        out_shape=jax.ShapeDtypeStruct(value.shape, value.dtype),
        in_specs=specs(pl.ANY, pl.ANY),
        out_specs=pl.BlockSpec(memory_space=pl.ANY),
        input_output_aliases={0: 0},
        compiler_params=pltpu.CompilerParams(vmem_limit_bytes=1024 * 1024),
    )(value, mark)


def by_core_kernel(first, second, out, _first, _second, sem):
    core = jnp.bitwise_and(lax.axis_index("fsdp"), 1)

    @pl.when(core == 1)
    def _():
        copy = pltpu.make_async_copy(first, out, sem)
        copy.start()
        copy.wait()

    @pl.when(core == 0)
    def _():
        copy = pltpu.make_async_copy(second, out, sem)
        copy.start()
        copy.wait()


def by_core(first, second):
    return pl.pallas_call(
        by_core_kernel,
        out_shape=(jax.ShapeDtypeStruct(first.shape, first.dtype),) * 3,
        in_specs=specs(pl.ANY, pl.ANY),
        out_specs=specs(pl.ANY, pl.ANY, pl.ANY),
        input_output_aliases={0: 1, 1: 2},
        scratch_shapes=[pltpu.SemaphoreType.DMA],
        compiler_params=pltpu.CompilerParams(vmem_limit_bytes=1024 * 1024),
    )(first, second)


def per_device(tokens, cotangent, w_blocks, blk_rows, blk_cols, counts):
    mine = pack(w_blocks, blk_rows, blk_cols, counts)
    by_x = [[place(z, x, c) for x in range(NX)] for z in range(NZ) for c in range(NC)]
    row = lax.all_gather(mine, "fsdp", axis=0, tiled=True, axis_index_groups=by_x)

    above, below = row, row
    held, moves = [row], [(0, 0)]
    for step in range(1, NZ // 2):
        above, below = up(above), down(below)
        held += [above, below]
        moves += [(-step, 0), (step, 0)]
    chosen, below, above = by_core(below, above)
    last = apart(chosen)
    held[-2:] = [above, below]
    stacks, rows = list(held), [[m] for m in moves]
    for part in (slice(0, 5), slice(5, 9), slice(9, 11)):
        stacks.append(sibling(jnp.concatenate(held[part], axis=0)))
        rows.append([(dz, 1) for dz, _ in moves[part]])
    dense, preact, mark = near(rows, stacks, tokens, cotangent.shape[1])
    last = after(last, mark)
    hidden, pieces = far(
        [[(NZ // 2, 0)], [(NZ // 2, 1)]],
        [last, sibling(last)],
        tokens,
        cotangent,
        preact,
        dense,
        lax.axis_size("tp"),
    )
    terms = lax.all_to_all(pieces, "tp", split_axis=0, concat_axis=0, tiled=True)
    summed = jnp.sum(terms.astype(jnp.float32), axis=0).astype(jnp.bfloat16)
    return (hidden, summed.T)


def solution(mesh):
    return jax.shard_map(
        per_device,
        mesh=mesh,
        in_specs=(
            P("fsdp", None),
            P("fsdp", "tp"),
            P("fsdp", "tp", None, None, None),
            P("fsdp", "tp", None),
            P("fsdp", "tp", None),
            P("fsdp", "tp"),
        ),
        out_specs=(P("fsdp", "tp"), P("fsdp", "tp")),
        check_vma=False,
    )
```
